512 devices in a mesh: front: 32 (over y, x, core), col: 16 (over z).
Axes of the slice: x: 4, y: 4, z: 16, core: 2. Of those that a mesh axis runs over, the one named last changes fastest.
Arguments:
- cases_one: float32 [192, 6144], P('front', 'col'), may hold values from -6 to 6
- cases_two: float32 [192, 10240], P('front', 'col'), may hold values from -6 to 6
- cases_parent: float32 [192, 16384], P('front', 'col'), may hold values from -6 to 6
- inverse_one: float32 [6144, 6144], P('front', 'col'), may hold values from -0.078125 to 0.078125
- inverse_two: float32 [10240, 10240], P('front', 'col'), may hold values from -0.0625 to 0.0625
- inverse_parent: float32 [16384, 16384], P('front', 'col'), may hold values from -0.046875 to 0.046875
- coupling_one: float32 [6144, 4096], P('front', 'col'), may hold values from -0.078125 to 0.078125
- coupling_two: float32 [10240, 8192], P('front', 'col'), may hold values from -0.0625 to 0.0625
- map_one: int32 [4096], replicated, may hold values from 0 to 16383, as said below
- map_two: int32 [8192], replicated, may hold values from 0 to 16383, as said below
Outputs:
- solution_one: float32 [192, 6144], P('front', 'col')
- solution_two: float32 [192, 10240], P('front', 'col')
- solution_parent: float32 [192, 16384], P('front', 'col')
The draws below stay inside these ranges and needn't reach their ends.
Inputs may be any that keep to these rules, and one draw needn't show every extreme that they name: `map_one`: entries are distinct. Each aligned block of 256 entries sends the same number of entries into each aligned range of 1024 parent rows. `map_two`: entries are distinct. Each aligned block of 512 entries sends the same number of entries into each aligned range of 1024 parent rows.
All inputs are finite; a program needn't handle non-finite values.
Results may differ from the reference program's by a relative error of at most 0.00013.
Values sent between devices are 32-bit elements; how exact they have to be, the bound alone decides.
A program may use at most 64 MiB of HBM per device.

```python
import jax
import jax.numpy as jnp
from jax import lax

P1 = 6144
P2 = 10240
PP = 16384
C1 = 4096
C2 = 8192
CASES = 192
OWN = 1024


def spread_rows(key, total):
    owners = PP // OWN
    width = total // owners
    share = width // owners
    source_keys = jax.random.split(jax.random.fold_in(key, total), owners)
    owner_keys = jax.random.split(jax.random.fold_in(key, total + 7), owners)

    def shuffle_width(single):
        return jax.random.permutation(single, width)

    def shuffle_owned(single):
        return jax.random.permutation(single, OWN)
    slots = jax.vmap(shuffle_width)(source_keys)
    places = jax.vmap(shuffle_owned)(owner_keys)
    target = slots % owners
    ranking = slots // owners
    source = jnp.arange(owners, dtype=jnp.int32)[:, None]
    local = places[target, source * share + ranking]
    return (target * OWN + local).reshape(total).astype(jnp.int32)


def draw_map_one(key, part):
    return spread_rows(key, C1)


def draw_map_two(key, part):
    return spread_rows(key, C2)


def levels(key, extent, shards, smallest, top_value):
    factor_of, own = 1.0, jax.random.fold_in(key, 6)
    for position, parts in shards:
        heights = jnp.exp(jax.random.uniform(jax.random.fold_in(own, position), (parts,), jnp.float32, smallest / len(shards), top_value / len(shards)))
        factor_of = factor_of * jnp.repeat(heights, extent[position] // parts).reshape([-1 if axis == position else 1 for axis in range(len(extent))])
    return factor_of


def normal_values(own_key, shape, deviation, bound, pieces=(), kind=jnp.bfloat16):
    drawn = jax.random.normal(own_key, shape, jnp.float32) * deviation
    if len(pieces) > 0:
        drawn = levels(own_key, shape, pieces, -0.22, 0.18) * drawn
    return jnp.clip(drawn, min=-bound, max=bound).astype(kind)


def setup_inputs(seed: int = 0) -> dict:
    splits = jax.random.split(jax.random.key(seed), 11)
    return {
        "cases_one": normal_values(splits[0], (CASES, P1), 1.0, 6.0, ((0, 32), (1, 16)), jnp.float32),
        "cases_two": normal_values(splits[1], (CASES, P2), 1.0, 6.0, ((0, 32), (1, 16)), jnp.float32),
        "cases_parent": normal_values(splits[2], (CASES, PP), 1.0, 6.0, ((0, 32), (1, 16)), jnp.float32),
        "inverse_one": normal_values(splits[3], (P1, P1), P1 ** -0.5, 0.078125, ((0, 32), (1, 16)), jnp.float32),
        "inverse_two": normal_values(splits[4], (P2, P2), P2 ** -0.5, 0.0625, ((0, 32), (1, 16)), jnp.float32),
        "inverse_parent": normal_values(splits[5], (PP, PP), PP ** -0.5, 0.046875, ((0, 32), (1, 16)), jnp.float32),
        "coupling_one": normal_values(splits[6], (P1, C1), P1 ** -0.5, 0.078125, ((0, 32), (1, 16)), jnp.float32),
        "coupling_two": normal_values(splits[7], (P2, C2), P2 ** -0.5, 0.0625, ((0, 32), (1, 16)), jnp.float32),
        "map_one": draw_map_one(jax.random.fold_in(splits[10], 71), 0),
        "map_two": draw_map_two(jax.random.fold_in(splits[10], 71), 0),
    }


def product(left, right):
    return jnp.dot(left, right, precision=lax.Precision.HIGHEST, preferred_element_type=jnp.float32)


def reference(cases_one, cases_two, cases_parent, inverse_one, inverse_two, inverse_parent, coupling_one, coupling_two, map_one, map_two):
    solved_one = product(cases_one, inverse_one.T)
    solved_two = product(cases_two, inverse_two.T)
    update_one = product(solved_one, coupling_one)
    update_two = product(solved_two, coupling_two)
    assembled = cases_parent.at[:, map_one].add(-update_one)
    assembled = assembled.at[:, map_two].add(-update_two)
    solved_parent = product(assembled, inverse_parent.T)
    solution_parent = product(solved_parent, inverse_parent)
    picked_one = solution_parent[:, map_one]
    picked_two = solution_parent[:, map_two]
    reduced_one = solved_one - product(picked_one, coupling_one.T)
    reduced_two = solved_two - product(picked_two, coupling_two.T)
    solution_one = product(reduced_one, inverse_one)
    solution_two = product(reduced_two, inverse_two)
    return solution_one, solution_two, solution_parent
```

```python
import functools

import jax
import jax.numpy as jnp
from jax import lax
from jax.experimental import pallas as pl
from jax.experimental.pallas import tpu as pltpu
from jax.sharding import PartitionSpec as P

MESH = pl.DeviceIdType.MESH
F32, BF16 = jnp.float32, jnp.bfloat16
CHIPS = [(dy, dx) for dy in range(4) for dx in range(4) if (dy, dx) != (0, 0)]
CHIPS.sort(key=lambda o: -(min(o[0], 4 - o[0]) + min(o[1], 4 - o[1])))
Z_ORDER = sorted(range(1, 16), key=lambda d: -min(d, 16 - d))


def split(value):
    high = value.astype(BF16)
    return high, (value - high.astype(F32)).astype(BF16)


def dot(left, right):
    return lax.dot_general(left, right, (((1,), (0,)), ((), ())), preferred_element_type=F32)


def dot_t(left, right):
    return lax.dot_general(left, right, (((1,), (1,)), ((), ())), preferred_element_type=F32)


def three(dot_fn, left, right):
    (lh, ll), (rh, rl) = left, right
    return dot_fn(lh, rh) + (dot_fn(lh, rl) + dot_fn(ll, rh))


def iota(shape, dim):
    return lax.broadcasted_iota(jnp.int32, shape, dim)


def scratch_plan():
    plan = {}
    vm = lambda *shape: pltpu.VMEM(shape, F32)
    half = lambda *shape: pltpu.VMEM(shape, BF16)
    dma = lambda *shape: pltpu.SemaphoreType.DMA(shape)
    for name, shape in (("io", (192, 384)), ("it", (320, 640)), ("ip", (512, 1024)), ("ko", (192, 256)), ("kt", (320, 512))):
        plan[name] = vm(*shape)
    plan["load"] = dma(5)
    for name in ("wc", "wp", "ck"):
        plan[name + "_h"] = half(512, 1024)
        plan[name + "_l"] = half(512, 1024)
    plan["ka_h"], plan["ka_l"] = half(256, 256), half(256, 256)
    plan["kb_h"], plan["kb_l"] = half(384, 512), half(384, 512)
    plan["sa"], plan["ra"] = vm(16, 16, 256), vm(16, 16, 256)
    plan["sb"], plan["rb"] = vm(16, 32, 384), vm(16, 32, 384)
    plan["sa_s"], plan["sa_r"] = dma(16), dma(16)
    plan["sb_s"], plan["sb_r"] = dma(16), dma(16)
    for i in range(3):
        plan[f"ag{i}"] = vm(16, 8, 1024)
        plan[f"x{i}"] = vm(2, 96, 1024)
        plan[f"ag{i}_s"], plan[f"ag{i}_r"] = dma(16), dma(16)
        plan[f"yp{i}"] = vm(4, 4, 48, 128)
        for n in ("na", "nb", "nc"):
            plan[f"{n}{i}"] = vm(4, 48, 128)
            plan[f"{n}{i}_s"], plan[f"{n}{i}_r"] = dma(4), dma(4)
        plan[f"fs{i}"], plan[f"fr{i}"] = vm(4, 48, 128), vm(4, 48, 128)
        plan[f"fs{i}_s"], plan[f"fs{i}_r"] = dma(4), dma(4)
        plan[f"g{i}"] = vm(4, 4, 48, 128)
        plan[f"gf{i}_s"], plan[f"gf{i}_r"] = dma(4), dma(4)
        for n in ("ga", "gb", "gc"):
            plan[f"{n}{i}_s"], plan[f"{n}{i}_r"] = dma(4), dma(4)
        plan[f"p{i}"] = vm(2, 96, 1024)
        plan[f"cr{i}"] = vm(96, 1024)
        plan[f"rs{i}"], plan[f"rr{i}"] = vm(16, 8, 1024), vm(16, 8, 1024)
        plan[f"rs{i}_s"], plan[f"rs{i}_r"] = dma(16), dma(16)
    return plan


PLAN = scratch_plan()
NAMES = list(PLAN)


def kernel(co, ct, cp, io, it, ip, ko, kt, m1, m2, out1, out2, outp, *scratch):
    r_ = dict(zip(NAMES, scratch))
    f, z = lax.axis_index("front"), lax.axis_index("col")
    core, chip = f % 2, f // 2
    x, y = chip % 4, chip // 4
    sent = []

    def copy(src, dst, send, recv, device):
        c = pltpu.make_async_remote_copy(
            src_ref=src, dst_ref=dst, send_sem=send, recv_sem=recv, device_id=device, device_id_type=MESH
        )
        c.start()
        sent.append(c)
        return c

    def at_chip(offset):
        other = ((y + offset[0]) % 4) * 4 + (x + offset[1]) % 4
        return other, (other * 2 + core, z)

    sibling = (chip * 2 + (1 - core), z)

    def at_z(step):
        return (f, (z + step + 16) % 16)

    loads = {}
    for i, (name, ref) in enumerate((("ko", ko), ("kt", kt), ("io", io), ("it", it), ("ip", ip))):
        loads[name] = pltpu.make_async_copy(ref, r_[name], r_["load"].at[i])
        loads[name].start()

    barrier = pltpu.get_barrier_semaphore()
    pl.semaphore_signal(barrier, inc=1, device_id=sibling, device_id_type=MESH)
    for o in CHIPS:
        pl.semaphore_signal(barrier, inc=1, device_id=at_chip(o)[1], device_id_type=MESH)
    for d in Z_ORDER:
        pl.semaphore_signal(barrier, inc=1, device_id=at_z(d), device_id_type=MESH)

    def sort_columns(mapped, width, source, rows, name):
        share = width // 16
        target = lax.shift_right_logical(mapped, 10)
        position = jnp.bitwise_and(mapped, 1023).astype(F32)
        marks = (iota((16, width), 0) == target).astype(F32)
        below = (iota((width, width), 0) < iota((width, width), 1)).astype(F32).astype(BF16)
        ranking = jnp.sum(dot(marks.astype(BF16), below) * marks, axis=0, keepdims=True)
        place = target * share + ranking.astype(jnp.int32)
        chosen = (iota((width, width), 0) == place).astype(F32).astype(BF16)
        high, low = r_[name + "_h"], r_[name + "_l"]
        high[0:rows, :], low[0:rows, :] = split(source[...])
        tail = jnp.where(iota((64, width), 0) == 0, position, 0.0)
        high[rows : rows + 64, :], low[rows : rows + 64, :] = split(tail)
        return dot_t(chosen, high[...]) + dot_t(chosen, low[...])

    loads["ko"].wait()
    r_["sa"][...] = sort_columns(m1[z], 256, r_["ko"], 192, "ka").reshape(16, 16, 256)
    loads["kt"].wait()
    r_["sb"][...] = sort_columns(m2[z], 512, r_["kt"], 320, "kb").reshape(16, 32, 384)

    ag0 = r_["ag0"]
    pad = jnp.zeros((2, 1024), F32)
    ag0[chip, 0:6, 0:384] = co[...]
    ag0[chip, 0:6, 384:1024] = ct[...]
    ag0[chip, 6:8, :] = pad

    pl.semaphore_wait(barrier, 31)

    def gather_start(i):
        buf = r_[f"ag{i}"]
        return [
            copy(buf.at[chip], buf.at[chip], r_[f"ag{i}_s"].at[k], r_[f"ag{i}_r"].at[k], at_chip(o)[1])
            for k, o in enumerate(CHIPS)
        ]

    def gather_end(i, copies):
        buf, xs = r_[f"ag{i}"], r_[f"x{i}"]
        for c in copies:
            c.wait_recv()
        for j in range(16):
            xs[0, 6 * j : 6 * j + 6, :] = buf[j, 0:6, :]
        copy(xs.at[0], xs.at[1], r_[f"ag{i}_s"].at[15], r_[f"ag{i}_r"].at[15], sibling).wait_recv()
        return xs[...].reshape(192, 1024)

    def share_start(i):
        yp, copies = r_[f"yp{i}"], []
        for o in (2, 1, 3, 0):
            q = (z // 4 + o) % 4
            for n, step in (("na", 1), ("nb", 15), ("nc", 2 + 12 * (q // 2))):
                sem = q
                copies.append(
                    (o, copy(yp.at[(z + step) % 4, q], r_[f"{n}{i}"].at[q], r_[f"{n}{i}_s"].at[sem], r_[f"{n}{i}_r"].at[sem], at_z(step)))
                )
        return copies

    def share_end(i, copies):
        yp, fs, fr, g = r_[f"yp{i}"], r_[f"fs{i}"], r_[f"fr{i}"], r_[f"g{i}"]
        r, q0 = z % 4, z // 4
        far, total = [], None
        for o in (2, 1, 3, 0):
            q = (q0 + o) % 4
            for k, c in copies:
                if k == o:
                    c.wait_recv()
            total = (yp[r, q] + r_[f"na{i}"][q]) + (r_[f"nb{i}"][q] + r_[f"nc{i}"][q])
            if o:
                fs[o] = total
                far.append(copy(fs.at[o], fr.at[o], r_[f"fs{i}_s"].at[o], r_[f"fs{i}_r"].at[o], at_z(4 * o)))
        for c in far:
            c.wait_recv()
        g[r, q0] = (total + fr[1]) + (fr[2] + fr[3])
        far = {
            o: copy(g.at[r, q0], g.at[r, q0], r_[f"gf{i}_s"].at[o], r_[f"gf{i}_r"].at[o], at_z(4 * o)) for o in (2, 1, 3)
        }
        near = []
        for o in (0, 1, 3, 2):
            q = (q0 - o + 4) % 4
            if o:
                far[o].wait_recv()
            for n, step in (("ga", 1), ("gb", 15), ("gc", 2 + 12 * (q // 2))):
                near.append(copy(g.at[r, q], g.at[r, q], r_[f"{n}{i}_s"].at[q], r_[f"{n}{i}_r"].at[q], at_z(step)))
        for c in near:
            c.wait_recv()
        return jnp.concatenate([g[k].reshape(192, 128) for k in range(4)], axis=1)

    def put_rows(i, value):
        for k in range(4):
            r_[f"yp{i}"][k] = value[:, 128 * k : 128 * k + 128].reshape(4, 48, 128)

    def reduce_front(i, value):
        p, cr, rs, rr = r_[f"p{i}"], r_[f"cr{i}"], r_[f"rs{i}"], r_[f"rr{i}"]
        p[...] = value.reshape(2, 96, 1024)
        copy(p.at[1], cr, r_[f"rs{i}_s"].at[15], r_[f"rs{i}_r"].at[15], sibling).wait_recv()
        for j in range(16):
            rs[j, 0:6, :] = p[0, 6 * j : 6 * j + 6, :] + cr[6 * j : 6 * j + 6, :]
            rs[j, 6:8, :] = pad
        copies = [
            copy(rs.at[at_chip(o)[0]], rr.at[k], r_[f"rs{i}_s"].at[k], r_[f"rs{i}_r"].at[k], at_chip(o)[1])
            for k, o in enumerate(CHIPS)
        ]
        total = rs[chip]
        for k, c in enumerate(copies):
            c.wait_recv()
            total = total + rr[k]
        return total

    first = gather_start(0)
    moved = []
    for n, d in enumerate(Z_ORDER):
        to = (z + d) % 16
        for name in ("a", "b"):
            s = r_["s" + name]
            moved.append(copy(s.at[to], r_["r" + name].at[z], r_[f"s{name}_s"].at[n], r_[f"s{name}_r"].at[n], at_z(d)))
    r_["ra"][z] = r_["sa"][z]
    r_["rb"][z] = r_["sb"][z]

    for name in ("wc_h", "wc_l"):
        r_[name][0:192, 384:1024] = jnp.zeros((192, 640), BF16)
        r_[name][192:512, 0:384] = jnp.zeros((320, 384), BF16)
    loads["io"].wait()
    r_["wc_h"][0:192, 0:384], r_["wc_l"][0:192, 0:384] = split(r_["io"][...])
    loads["it"].wait()
    r_["wc_h"][192:512, 384:1024], r_["wc_l"][192:512, 384:1024] = split(r_["it"][...])
    loads["ip"].wait()
    r_["wp_h"][...], r_["wp_l"][...] = split(r_["ip"][...])
    pair = lambda name: (r_[name + "_h"][...], r_[name + "_l"][...])

    cases = gather_end(0, first)
    put_rows(0, three(dot_t, split(cases), pair("wc")))
    near = share_start(0)

    solved = share_end(0, near)

    for c in moved:
        c.wait_recv()
    for name, width, lanes, rows, start in (("ra", 256, 256, 192, 0), ("rb", 512, 384, 320, 192)):
        got = r_[name][...].reshape(width, lanes)
        land = (iota((width, 1024), 1) == got[:, rows : rows + 1].astype(jnp.int32)).astype(F32).astype(BF16)
        high, low = split(got.T)
        r_["ck_h"][start : start + rows, :] = dot(high[0:rows], land).astype(BF16)
        r_["ck_l"][start : start + rows, :] = dot(low[0:rows], land).astype(BF16)

    updated = reduce_front(0, three(dot, split(solved), pair("ck")))

    ag1 = r_["ag1"]
    ag1[chip, 0:6, :] = cp[...] - updated[0:6]
    ag1[chip, 6:8, :] = pad
    assembled = gather_end(1, gather_start(1))
    put_rows(1, three(dot_t, split(assembled), pair("wp")))
    solved_parent = share_end(1, share_start(1))
    parent = reduce_front(1, three(dot, split(solved_parent), pair("wp")))
    outp[...] = parent[0:6]
    r_["ag2"][chip] = parent

    parents = gather_end(2, gather_start(2))
    put_rows(2, three(dot_t, split(parents), pair("ck")))
    lifted = share_end(2, share_start(2))
    solved = jnp.concatenate([r_["g0"][k].reshape(192, 128) for k in range(4)], axis=1)
    last = reduce_front(2, three(dot, split(solved - lifted), pair("wc")))
    out1[...] = last[0:6, 0:384]
    out2[...] = last[0:6, 384:1024]

    for c in sent:
        c.wait_send()


def local(co, ct, cp, io, it, ip, ko, kt, m1, m2):
    vmem, hbm = pl.BlockSpec(memory_space=pltpu.VMEM), pl.BlockSpec(memory_space=pl.ANY)
    shape = lambda like: jax.ShapeDtypeStruct(like.shape, F32)
    return tuple(
        pl.pallas_call(
            kernel,
            name="fronts",
            out_shape=(shape(co), shape(ct), shape(cp)),
            in_specs=[vmem] * 3 + [hbm] * 5 + [vmem] * 2,
            out_specs=(vmem,) * 3,
            scratch_shapes=[PLAN[n] for n in NAMES],
            compiler_params=pltpu.CompilerParams(
                collective_id=1, has_side_effects=True, vmem_limit_bytes=58 * 2**20
            ),
        )(co, ct, cp, io, it, ip, ko, kt, m1.reshape(16, 1, 256), m2.reshape(16, 1, 512))
    )


def solution(mesh):
    block = P("front", "col")
    return jax.shard_map(
        local,
        mesh=mesh,
        in_specs=(block,) * 8 + (P(), P()),
        out_specs=(block,) * 3,
        check_vma=False,
    )
```

```python
import functools

import jax
import jax.numpy as jnp
from jax import lax
from jax.experimental import pallas as pl
from jax.experimental.pallas import tpu as pltpu
from jax.sharding import PartitionSpec as P

MESH = pl.DeviceIdType.MESH
F32, BF16 = jnp.float32, jnp.bfloat16
CHIPS = [(dy, dx) for dy in range(4) for dx in range(4) if (dy, dx) != (0, 0)]
CHIPS.sort(key=lambda o: -(min(o[0], 4 - o[0]) + min(o[1], 4 - o[1])))
Z_ORDER = sorted(range(1, 16), key=lambda d: -min(d, 16 - d))


def split(value):
    high = value.astype(BF16)
    return high, (value - high.astype(F32)).astype(BF16)


def dot(left, right):
    return lax.dot_general(left, right, (((1,), (0,)), ((), ())), preferred_element_type=F32)


def dot_t(left, right):
    return lax.dot_general(left, right, (((1,), (1,)), ((), ())), preferred_element_type=F32)


def three(dot_fn, left, right):
    (lh, ll), (rh, rl) = left, right
    return dot_fn(lh, rh) + (dot_fn(lh, rl) + dot_fn(ll, rh))


def iota(shape, dim):
    return lax.broadcasted_iota(jnp.int32, shape, dim)


def scratch_plan():
    plan = {}
    vm = lambda *shape: pltpu.VMEM(shape, F32)
    half = lambda *shape: pltpu.VMEM(shape, BF16)
    dma = lambda *shape: pltpu.SemaphoreType.DMA(shape)
    for name, shape in (("io", (192, 384)), ("it", (320, 640)), ("ip", (512, 1024)), ("ko", (192, 256)), ("kt", (320, 512))):
        plan[name] = vm(*shape)
    plan["load"] = dma(5)
    for name, shape in (("wc", (512, 1024)), ("wp", (512, 1024)), ("kc", (512, 768))):
        plan[name + "_h"] = half(*shape)
        plan[name + "_l"] = half(*shape)
    plan["c1"], plan["c2"], plan["land"] = half(256, 256), half(512, 512), half(1024, 768)
    for n in ("ti", "tu", "tb"):
        plan[n], plan[n + "g"] = vm(16, 8, 128), vm(16, 8, 128)
        plan[n + "_s"], plan[n + "_r"] = dma(16), dma(16)
    for i, (there, back) in enumerate(((1024, 768), (1024, 1024), (768, 1024))):
        plan[f"ag{i}"], plan[f"x{i}"] = vm(16, 6, there), vm(2, 96, there)
        plan[f"ag{i}_s"], plan[f"ag{i}_r"] = dma(16), dma(16)
        for h in (0, 1):
            j = f"{i}{h}"
            plan["yp" + j], plan["g" + j] = vm(16, 24, 128), vm(16, 24, 128)
            plan["nr" + j], plan["n3" + j] = vm(4, 3, 24, 128), vm(24, 128)
            plan[f"nr{j}_s"], plan[f"nr{j}_r"] = dma(4, 3), dma(4, 3)
            plan["fs" + j], plan["fr" + j] = vm(3, 24, 128), vm(3, 24, 128)
            plan[f"fs{j}_s"], plan[f"fs{j}_r"] = dma(3), dma(3)
            plan[f"gf{j}_s"], plan[f"gf{j}_r"] = dma(3), dma(3)
            plan[f"gn{j}_s"], plan[f"gn{j}_r"] = dma(4, 3), dma(4, 3)
            plan[f"l{j}_s"], plan[f"l{j}_r"] = dma(2), dma(2)
        plan[f"p{i}"], plan[f"cr{i}"] = vm(2, 96, back), vm(96, back)
        plan[f"rs{i}"], plan[f"rr{i}"] = vm(16, 6, back), vm(16, 6, back)
        plan[f"rs{i}_s"], plan[f"rs{i}_r"] = dma(16), dma(16)
    return plan


PLAN = scratch_plan()
NAMES = list(PLAN)


def kernel(co, ct, cp, io, it, ip, ko, kt, m1, m2, out, *scratch):
    r_ = dict(zip(NAMES, scratch))
    f, z = lax.axis_index("front"), lax.axis_index("col")
    core, chip = f % 2, f // 2
    x, y = chip % 4, chip // 4
    sent = []

    def copy(src, dst, send, recv, device):
        c = pltpu.make_async_remote_copy(
            src_ref=src, dst_ref=dst, send_sem=send, recv_sem=recv, device_id=device, device_id_type=MESH
        )
        c.start()
        sent.append(c)
        return c

    def at_chip(offset):
        other = ((y + offset[0]) % 4) * 4 + (x + offset[1]) % 4
        return other, (other * 2 + core, z)

    sibling = (chip * 2 + (1 - core), z)

    def at_z(step):
        return (f, (z + step + 16) % 16)

    loads = {}
    for i, (name, ref) in enumerate((("ko", ko), ("kt", kt), ("io", io), ("it", it), ("ip", ip))):
        loads[name] = pltpu.make_async_copy(ref, r_[name], r_["load"].at[i])
        loads[name].start()

    barrier = pltpu.get_barrier_semaphore()
    pl.semaphore_signal(barrier, inc=1, device_id=sibling, device_id_type=MESH)
    for o in CHIPS:
        pl.semaphore_signal(barrier, inc=1, device_id=at_chip(o)[1], device_id_type=MESH)
    for d in Z_ORDER:
        pl.semaphore_signal(barrier, inc=1, device_id=at_z(d), device_id_type=MESH)

    def order(mapped, width, name):
        share = width // 16
        target = lax.shift_right_logical(mapped, 10)
        marks = (iota((16, width), 0) == target).astype(F32)
        below = (iota((width, width), 0) < iota((width, width), 1)).astype(F32).astype(BF16)
        ranking = jnp.sum(dot(marks.astype(BF16), below) * marks, axis=0, keepdims=True)
        place = target * share + ranking.astype(jnp.int32)
        r_[name][...] = (iota((width, width), 0) == place).astype(F32).astype(BF16)
        position = jnp.bitwise_and(mapped, 1023).astype(F32)
        return jnp.where(iota((8, width), 0) == 0, position, 0.0)

    def exact(dot_fn, value, name):
        high = value.astype(BF16).astype(F32)
        both = dot_fn(jnp.concatenate([high, value - high], axis=0).astype(BF16), r_[name][...])
        return both[0:8] + both[8:16]

    def exchange(n):
        tiles = r_[n]
        r_[n + "g"][z] = tiles[z]
        return [
            copy(tiles.at[(z + d) % 16], r_[n + "g"].at[z], r_[n + "_s"].at[k], r_[n + "_r"].at[k], at_z(d))
            for k, d in enumerate(Z_ORDER)
        ]

    def to_owners(n, one, two):
        tiles = r_[n]
        for value, name, share, at in ((one, "c1", 16, 0), (two, "c2", 32, 16)):
            ordered = exact(dot_t, value, name)
            for d in range(16):
                tiles[d, :, at : at + share] = ordered[:, share * d : share * d + share]
        return exchange(n)

    def pieces(n, copies, start, stop):
        return jnp.concatenate([r_[n + "g"][k][:, start:stop] for k in range(16)], axis=1)

    ag0 = r_["ag0"]
    ag0[chip, :, 0:384] = co[...]
    ag0[chip, :, 384:1024] = ct[...]
    index_one = order(m1[z], 256, "c1")
    index_two = order(m2[z], 512, "c2")

    pl.semaphore_wait(barrier, 31)

    def gather_start(i):
        buf = r_[f"ag{i}"]
        return [
            copy(buf.at[chip], buf.at[chip], r_[f"ag{i}_s"].at[k], r_[f"ag{i}_r"].at[k], at_chip(o)[1])
            for k, o in enumerate(CHIPS)
        ]

    def gather_end(i, copies):
        buf, xs = r_[f"ag{i}"], r_[f"x{i}"]
        for c in copies:
            c.wait_recv()
        for j in range(16):
            xs[0, 6 * j : 6 * j + 6, :] = buf[j]
        return copy(xs.at[0], xs.at[1], r_[f"ag{i}_s"].at[15], r_[f"ag{i}_r"].at[15], sibling)

    NEAR = (2, 14, 1, 15)
    odd = z % 2
    opposite = 3 - 6 * odd

    def on(t):
        return 15 - 10 * t if not isinstance(t, int) else (0, 5, -5)[t]

    def share_start(i, value):
        yp = r_["yp" + i]
        for k in range(4):
            yp[4 * k : 4 * k + 4] = value[:, 128 * k : 128 * k + 128].reshape(4, 24, 128)
        last = copy(yp.at[(z + 8) % 16], r_["n3" + i], r_[f"l{i}_s"].at[0], r_[f"l{i}_r"].at[0], at_z(opposite))
        near = []
        for t in (1, 2, 0):
            for k, n in enumerate(NEAR):
                near.append(copy(yp.at[(z + n + on(t) + 16) % 16], r_["nr" + i].at[k, t], r_[f"nr{i}_s"].at[k, t], r_[f"nr{i}_r"].at[k, t], at_z(n)))
        return near, last

    def share(i, copies):
        yp, nr, fs, fr, g = r_["yp" + i], r_["nr" + i], r_["fs" + i], r_["fr" + i], r_["g" + i]
        near, last = copies
        yield
        for c in near[:8]:
            c.wait_recv()
        far = []
        for t in (1 + odd, 2 - odd):
            step = on(t)
            total = yp[(z + step + 16) % 16] + ((nr[0, t] + nr[1, t]) + (nr[2, t] + nr[3, t]))
            if far:
                last.wait_recv()
                total = total + r_["n3" + i][...]
            fs[t] = total
            far.append(copy(fs.at[t], fr.at[t], r_[f"fs{i}_s"].at[t], r_[f"fs{i}_r"].at[t], at_z(step)))
        yield
        for c in near[8:]:
            c.wait_recv()
        total = yp[z] + ((nr[0, 0] + nr[1, 0]) + (nr[2, 0] + nr[3, 0]))
        for c in far:
            c.wait_recv()
        g[z] = total + (fr[1] + fr[2])
        far = [copy(g.at[z], g.at[z], r_[f"gf{i}_s"].at[t], r_[f"gf{i}_r"].at[t], at_z(on(t))) for t in (1, 2)]

        def forward(t, block):
            return [
                copy(g.at[block], g.at[block], r_[f"gn{i}_s"].at[k, t], r_[f"gn{i}_r"].at[k, t], at_z(n))
                for k, n in enumerate(NEAR)
            ]

        near = forward(0, z)
        yield
        for c in far:
            c.wait_recv()
        block = (z - on(1 + odd) + 16) % 16
        near.append(copy(g.at[block], g.at[block], r_[f"l{i}_s"].at[1], r_[f"l{i}_r"].at[1], at_z(opposite)))
        for t in (1, 2):
            near += forward(t, (z - on(t) + 16) % 16)
        yield
        for c in near:
            c.wait_recv()

    def shared(i):
        g = r_["g" + i]
        return jnp.concatenate([g[4 * k : 4 * k + 4].reshape(96, 128) for k in range(4)], axis=1)

    def stage(i, first, there, meanwhile, take, back):
        xs, p, cr, rs, rr = r_[f"x{i}"], r_[f"p{i}"], r_[f"cr{i}"], r_[f"rs{i}"], r_[f"rr{i}"]
        across = gather_end(i, first)
        left = share(f"{i}0", share_start(f"{i}0", there(xs[0])))
        next(left)
        across.wait_recv()
        right = share(f"{i}1", share_start(f"{i}1", there(xs[1])))
        meanwhile()
        next(right)
        for _ in range(3):
            next(left)
            next(right)
        for _ in left:
            pass
        p[0] = back(take(shared(f"{i}0"), 0))
        for _ in right:
            pass
        p[1] = back(take(shared(f"{i}1"), 1))
        copy(p.at[1], cr, r_[f"rs{i}_s"].at[15], r_[f"rs{i}_r"].at[15], sibling).wait_recv()
        for j in range(16):
            rs[j] = p[0, 6 * j : 6 * j + 6, :] + cr[6 * j : 6 * j + 6, :]
        copies = [
            copy(rs.at[at_chip(o)[0]], rr.at[k], r_[f"rs{i}_s"].at[k], r_[f"rs{i}_r"].at[k], at_chip(o)[1])
            for k, o in enumerate(CHIPS)
        ]
        total = rs[chip]
        for k, c in enumerate(copies):
            c.wait_recv()
            total = total + rr[k]
        return total

    first = gather_start(0)
    indices = to_owners("ti", index_one, index_two)
    pair = lambda name: (r_[name + "_h"][...], r_[name + "_l"][...])
    product = lambda dot_fn, name: lambda value: three(dot_fn, split(value), pair(name))
    eight = lambda value: jnp.concatenate([value, jnp.zeros((2, value.shape[1]), F32)], axis=0)

    for name in ("wc_h", "wc_l"):
        r_[name][0:192, 384:1024] = jnp.zeros((192, 640), BF16)
        r_[name][192:512, 0:384] = jnp.zeros((320, 384), BF16)
    loads["io"].wait()
    r_["wc_h"][0:192, 0:384], r_["wc_l"][0:192, 0:384] = split(r_["io"][...])
    loads["it"].wait()
    r_["wc_h"][192:512, 384:1024], r_["wc_l"][192:512, 384:1024] = split(r_["it"][...])

    def prepare():
        loads["ko"].wait()
        loads["kt"].wait()
        r_["kc_h"][0:192, 0:256], r_["kc_l"][0:192, 0:256] = split(r_["ko"][...])
        r_["kc_h"][192:512, 256:768], r_["kc_l"][192:512, 256:768] = split(r_["kt"][...])
        for n in ("kc_h", "kc_l"):
            r_[n][0:192, 256:768] = jnp.zeros((192, 512), BF16)
            r_[n][192:512, 0:256] = jnp.zeros((320, 256), BF16)

    updated = stage(0, first, product(dot_t, "wc"), prepare, lambda value, h: value, product(dot, "kc"))
    moved = to_owners("tu", eight(updated[:, 0:256]), eight(updated[:, 256:768]))
    for c in indices:
        c.wait_recv()
    landing = pieces("ti", indices, 0, 48)
    r_["land"][...] = (iota((1024, 768), 0) == landing[0:1, :].astype(jnp.int32)).astype(F32).astype(BF16)
    for c in moved:
        c.wait_recv()
    arrived = exact(dot_t, pieces("tu", moved, 0, 48), "land")

    r_["ag1"][chip] = cp[...] - arrived[0:6]
    first = gather_start(1)
    loads["ip"].wait()
    r_["wp_h"][...], r_["wp_l"][...] = split(r_["ip"][...])
    parent = stage(1, first, product(dot_t, "wp"), lambda: None, lambda value, h: value, product(dot, "wp"))
    out[:, 1024:2048] = parent

    picked = exact(dot, eight(parent), "land")
    for d in range(16):
        r_["tb"][d, :, 0:48] = picked[:, 48 * d : 48 * d + 48]
    moved = exchange("tb")
    for c in moved:
        c.wait_recv()
    r_["ag2"][chip, :, 0:256] = exact(dot, pieces("tb", moved, 0, 16), "c1")[0:6]
    r_["ag2"][chip, :, 256:768] = exact(dot, pieces("tb", moved, 16, 48), "c2")[0:6]
    first = gather_start(2)
    reduced = lambda value, h: shared(f"0{h}") - value
    out[:, 0:1024] = stage(2, first, product(dot_t, "kc"), lambda: None, reduced, product(dot, "wc"))

    for c in sent:
        c.wait_send()


def local(co, ct, cp, io, it, ip, ko, kt, m1, m2):
    vmem, hbm = pl.BlockSpec(memory_space=pltpu.VMEM), pl.BlockSpec(memory_space=pl.ANY)
    whole = pl.pallas_call(
        kernel,
        name="fronts",
        out_shape=jax.ShapeDtypeStruct((6, 2048), F32),
        in_specs=[vmem] * 3 + [hbm] * 5 + [vmem] * 2,
        out_specs=vmem,
        scratch_shapes=[PLAN[n] for n in NAMES],
        compiler_params=pltpu.CompilerParams(collective_id=1, has_side_effects=True, vmem_limit_bytes=58 * 2**20),
    )(co, ct, cp, io, it, ip, ko, kt, m1.reshape(16, 1, 256), m2.reshape(16, 1, 512))
    return whole[:, 0:384], whole[:, 384:1024], whole[:, 1024:2048]


def solution(mesh):
    block = P("front", "col")
    return jax.shard_map(
        local,
        mesh=mesh,
        in_specs=(block,) * 8 + (P(), P()),
        out_specs=(block,) * 3,
        check_vma=False,
    )
```

```python
import functools

import jax
import jax.numpy as jnp
from jax import lax
from jax.experimental import pallas as pl
from jax.experimental.pallas import tpu as pltpu
from jax.sharding import PartitionSpec as P

MESH = pl.DeviceIdType.MESH
F32, BF16 = jnp.float32, jnp.bfloat16
CHIPS = [(dy, dx) for dy in range(4) for dx in range(4) if (dy, dx) != (0, 0)]
CHIPS.sort(key=lambda o: -(min(o[0], 4 - o[0]) + min(o[1], 4 - o[1])))
Z_ORDER = sorted(range(1, 16), key=lambda d: -min(d, 16 - d))


def split(value):
    high = value.astype(BF16)
    return high, (value - high.astype(F32)).astype(BF16)


def dot(left, right):
    return lax.dot_general(left, right, (((1,), (0,)), ((), ())), preferred_element_type=F32)


def dot_t(left, right):
    return lax.dot_general(left, right, (((1,), (1,)), ((), ())), preferred_element_type=F32)


def three(dot_fn, left, right):
    (lh, ll), (rh, rl) = left, right
    rows = lh.shape[0]
    both = dot_fn(jnp.concatenate([lh, ll], axis=0), rh)
    return both[0:rows] + (both[rows : 2 * rows] + dot_fn(lh, rl))


def iota(shape, dim):
    return lax.broadcasted_iota(jnp.int32, shape, dim)


def scratch_plan():
    plan = {}
    vm = lambda *shape: pltpu.VMEM(shape, F32)
    half = lambda *shape: pltpu.VMEM(shape, BF16)
    dma = lambda *shape: pltpu.SemaphoreType.DMA(shape)
    for name, shape in (("io", (192, 384)), ("it", (320, 640)), ("ip", (512, 1024)), ("ko", (192, 256)), ("kt", (320, 512))):
        plan[name] = vm(*shape)
    plan["cp"], plan["m1"], plan["m2"] = vm(6, 1024), pltpu.VMEM((1, 256), jnp.int32), pltpu.VMEM((1, 512), jnp.int32)
    plan["load"] = dma(10)
    for name, shape in (("wc", (512, 1024)), ("wp", (512, 1024)), ("kc", (512, 768))):
        plan[name + "_h"] = half(*shape)
        plan[name + "_l"] = half(*shape)
    plan["c1"], plan["c2"], plan["land"] = half(256, 256), half(512, 512), half(1024, 768)
    for n in ("ti", "tu", "tb"):
        plan[n], plan[n + "g"] = vm(16, 8, 128), vm(16, 8, 128)
        plan[n + "_s"], plan[n + "_r"] = dma(16), dma(16)
    for i, (there, back) in enumerate(((1024, 768), (1024, 1024), (768, 1024))):
        plan[f"ag{i}"], plan[f"x{i}"] = vm(16, 6, there), vm(2, 96, there)
        plan[f"ag{i}_s"], plan[f"ag{i}_r"] = dma(16), dma(16)
        for h in (0, 1):
            j = f"{i}{h}"
            plan["yp" + j], plan["g" + j] = vm(16, 24, 128), vm(16, 24, 128)
            plan["ns" + j], plan["nr" + j], plan["n3" + j] = vm(4, 3, 24, 128), vm(4, 3, 24, 128), vm(24, 128)
            plan["fs" + j], plan["f5" + j], plan["f10" + j] = vm(3, 24, 128), vm(2, 2, 24, 128), vm(2, 24, 128)
            plan["gs" + j], plan["gr" + j] = vm(3, 24, 128), vm(4, 3, 24, 128)
            for n, count in (("n", 5), ("f", 4), ("b", 5)):
                plan[f"{n}{j}_s"], plan[f"{n}{j}_r"] = dma(count), dma(count)
        plan[f"p{i}"], plan[f"cr{i}"] = vm(2, 96, back), vm(96, back)
        plan[f"rs{i}"], plan[f"rr{i}"] = vm(16, 6, back), vm(16, 6, back)
        plan[f"rs{i}_s"], plan[f"rs{i}_r"] = dma(16), dma(16)
        plan[f"cr{i}_s"], plan[f"cr{i}_r"] = dma(4), dma(4)
    return plan


PLAN = scratch_plan()
NAMES = list(PLAN)


def kernel(co, ct, cp, io, it, ip, ko, kt, m1, m2, out, *scratch):
    r_ = dict(zip(NAMES, scratch))
    f, z = lax.axis_index("front"), lax.axis_index("col")
    core, chip = f % 2, f // 2
    x, y = chip % 4, chip // 4
    sent = []

    def copy(src, dst, send, recv, device):
        c = pltpu.make_async_remote_copy(
            src_ref=src, dst_ref=dst, send_sem=send, recv_sem=recv, device_id=device, device_id_type=MESH
        )
        c.start()
        sent.append(c)
        return c

    def at_chip(offset):
        other = ((y + offset[0]) % 4) * 4 + (x + offset[1]) % 4
        return other, (other * 2 + core, z)

    pair = lambda name: (r_[name + "_h"][...], r_[name + "_l"][...])
    sibling = (chip * 2 + (1 - core), z)

    def at_z(step):
        return (f, (z + step + 16) % 16)

    barrier = pltpu.get_barrier_semaphore()
    pl.semaphore_signal(barrier, inc=1, device_id=sibling, device_id_type=MESH)
    for o in CHIPS:
        pl.semaphore_signal(barrier, inc=1, device_id=at_chip(o)[1], device_id_type=MESH)
    for d in Z_ORDER:
        pl.semaphore_signal(barrier, inc=1, device_id=at_z(d), device_id_type=MESH)

    loads = {}
    ag0 = r_["ag0"]
    for i, (name, ref, to) in enumerate(
        (
            ("co", co, ag0.at[chip, :, 0:384]),
            ("ct", ct, ag0.at[chip, :, 384:1024]),
            ("m1", m1.at[z], r_["m1"]),
            ("m2", m2.at[z], r_["m2"]),
            ("io", io, r_["io"]),
            ("it", it, r_["it"]),
            ("ko", ko, r_["ko"]),
            ("kt", kt, r_["kt"]),
            ("cp", cp, r_["cp"]),
            ("ip", ip, r_["ip"]),
        )
    ):
        loads[name] = pltpu.make_async_copy(ref, to, r_["load"].at[i])
        loads[name].start()

    def order(mapped, width, name):
        share = width // 16
        target = lax.shift_right_logical(mapped, 10)
        marks = (iota((16, width), 0) == target).astype(F32)
        below = (iota((width, width), 0) < iota((width, width), 1)).astype(F32).astype(BF16)
        ranking = jnp.sum(dot(marks.astype(BF16), below) * marks, axis=0, keepdims=True)
        place = target * share + ranking.astype(jnp.int32)
        r_[name][...] = (iota((width, width), 0) == place).astype(F32).astype(BF16)
        position = jnp.bitwise_and(mapped, 1023).astype(F32)
        return jnp.where(iota((8, width), 0) == 0, position, 0.0)

    def exact(dot_fn, value, name):
        high = value.astype(BF16).astype(F32)
        both = dot_fn(jnp.concatenate([high, value - high], axis=0).astype(BF16), r_[name][...])
        return both[0:8] + both[8:16]

    def exchange(n):
        tiles = r_[n]
        r_[n + "g"][z] = tiles[z]
        return [
            copy(tiles.at[(z + d) % 16], r_[n + "g"].at[z], r_[n + "_s"].at[k], r_[n + "_r"].at[k], at_z(d))
            for k, d in enumerate(Z_ORDER)
        ]

    def to_owners(n, one, two):
        tiles = r_[n]
        for value, name, share, at in ((one, "c1", 16, 0), (two, "c2", 32, 16)):
            ordered = exact(dot_t, value, name)
            for d in range(16):
                tiles[d, :, at : at + share] = ordered[:, share * d : share * d + share]
        return exchange(n)

    def pieces(n, copies, start, stop):
        return jnp.concatenate([r_[n + "g"][k][:, start:stop] for k in range(16)], axis=1)

    loads["m1"].wait()
    loads["m2"].wait()
    index_one = order(r_["m1"][...], 256, "c1")
    index_two = order(r_["m2"][...], 512, "c2")
    loads["co"].wait()
    loads["ct"].wait()

    pl.semaphore_wait(barrier, 31)

    def gather_start(i):
        buf = r_[f"ag{i}"]
        return [
            copy(buf.at[chip], buf.at[chip], r_[f"ag{i}_s"].at[k], r_[f"ag{i}_r"].at[k], at_chip(o)[1])
            for k, o in enumerate(CHIPS)
        ]

    def gather_end(i, copies):
        buf, xs = r_[f"ag{i}"], r_[f"x{i}"]
        for c in copies:
            c.wait_recv()
        for j in range(16):
            xs[0, 6 * j : 6 * j + 6, :] = buf[j]
        return copy(xs.at[0], xs.at[1], r_[f"ag{i}_s"].at[15], r_[f"ag{i}_r"].at[15], sibling)

    NEAR = (2, 14, 1, 15)
    odd = z % 2
    opposite = 3 - 6 * odd

    def block(step, j):
        return (z + step + 5 * (j - 1) + 32) % 16

    def share_start(i, value):
        yp = r_["yp" + i]
        for k in range(4):
            yp[4 * k : 4 * k + 4] = value[:, 128 * k : 128 * k + 128].reshape(4, 24, 128)
        ns, nr = r_["ns" + i], r_["nr" + i]
        sems = lambda k: (r_[f"n{i}_s"].at[k], r_[f"n{i}_r"].at[k])
        near = [copy(yp.at[(z + 8) % 16], r_["n3" + i], *sems(4), at_z(opposite))]
        for k, n in enumerate(NEAR):
            for j in range(3):
                ns[k, j] = yp[block(n, j)]
            near.append(copy(ns.at[k], nr.at[k], *sems(k), at_z(n)))
        return near

    def share(i, near):
        yp, nr, fs, f5, f10 = r_["yp" + i], r_["nr" + i], r_["fs" + i], r_["f5" + i], r_["f10" + i]
        g, gs, gr = r_["g" + i], r_["gs" + i], r_["gr" + i]
        yield
        for c in near:
            c.wait_recv()
        for j in range(3):
            fs[j] = yp[block(0, j)] + ((nr[0, j] + nr[1, j]) + (nr[2, j] + nr[3, j]))
        fs[2 * odd] = fs[2 * odd] + r_["n3" + i][...]
        sems = lambda k: (r_[f"f{i}_s"].at[k], r_[f"f{i}_r"].at[k])
        far = [
            copy(fs.at[2], f10.at[0], *sems(0), at_z(10)),
            copy(fs.at[0], f10.at[1], *sems(1), at_z(-10)),
            copy(fs.at[pl.ds(1, 2)], f5.at[0], *sems(2), at_z(5)),
            copy(fs.at[pl.ds(0, 2)], f5.at[1], *sems(3), at_z(-5)),
        ]
        yield
        for c in far:
            c.wait_recv()
        gs[0] = fs[0] + (f5[0, 0] + f10[0])
        gs[1] = fs[1] + (f5[0, 1] + f5[1, 0])
        gs[2] = fs[2] + (f5[1, 1] + f10[1])
        sent_sems = lambda k: (r_[f"b{i}_s"].at[k], r_[f"b{i}_r"].at[k])
        near = [copy(gs.at[2 * odd], g.at[block(0, 2 * odd)], *sent_sems(4), at_z(opposite))]
        near += [copy(gs, gr.at[k], *sent_sems(k), at_z(n)) for k, n in enumerate(NEAR)]
        for j in range(3):
            g[block(0, j)] = gs[j]
        yield
        for c in near:
            c.wait_recv()
        for k, n in enumerate(NEAR):
            for j in range(3):
                g[block(-n, j)] = gr[k, j]

    def shared(i):
        g = r_["g" + i]
        return jnp.concatenate([g[4 * k : 4 * k + 4].reshape(96, 128) for k in range(4)], axis=1)

    def stage(i, first, there, meanwhile, take, back):
        xs, p, cr, rs, rr = r_[f"x{i}"], r_[f"p{i}"], r_[f"cr{i}"], r_[f"rs{i}"], r_[f"rr{i}"]
        across = gather_end(i, first)
        left = share(f"{i}0", share_start(f"{i}0", there(xs[0])))
        next(left)
        across.wait_recv()
        right = share(f"{i}1", share_start(f"{i}1", there(xs[1])))
        meanwhile()
        next(right)
        for _ in range(2):
            next(left)
            next(right)
        for _ in left:
            pass
        p[0] = three(dot, split(take(shared(f"{i}0"), 0)), pair(back))
        for _ in right:
            pass
        value, across = split(take(shared(f"{i}1"), 1)), []
        for c in range(p.shape[2] // 256):
            part = (slice(None), slice(256 * c, 256 * c + 256))
            p[(1,) + part] = three(dot, value, (r_[back + "_h"][part], r_[back + "_l"][part]))
            across.append(copy(p.at[(1,) + part], cr.at[part], r_[f"cr{i}_s"].at[c], r_[f"cr{i}_r"].at[c], sibling))
        for c in across:
            c.wait_recv()
        for j in range(16):
            rs[j] = p[0, 6 * j : 6 * j + 6, :] + cr[6 * j : 6 * j + 6, :]
        copies = [
            copy(rs.at[at_chip(o)[0]], rr.at[k], r_[f"rs{i}_s"].at[k], r_[f"rs{i}_r"].at[k], at_chip(o)[1])
            for k, o in enumerate(CHIPS)
        ]
        total = rs[chip]
        for k, c in enumerate(copies):
            c.wait_recv()
            total = total + rr[k]
        return total

    first = gather_start(0)
    indices = to_owners("ti", index_one, index_two)
    product = lambda dot_fn, name: lambda value: three(dot_fn, split(value), pair(name))
    eight = lambda value: jnp.concatenate([value, jnp.zeros((2, value.shape[1]), F32)], axis=0)

    for name in ("wc_h", "wc_l"):
        r_[name][0:192, 384:1024] = jnp.zeros((192, 640), BF16)
        r_[name][192:512, 0:384] = jnp.zeros((320, 384), BF16)
    loads["io"].wait()
    r_["wc_h"][0:192, 0:384], r_["wc_l"][0:192, 0:384] = split(r_["io"][...])
    loads["it"].wait()
    r_["wc_h"][192:512, 384:1024], r_["wc_l"][192:512, 384:1024] = split(r_["it"][...])

    def prepare():
        loads["ko"].wait()
        loads["kt"].wait()
        r_["kc_h"][0:192, 0:256], r_["kc_l"][0:192, 0:256] = split(r_["ko"][...])
        r_["kc_h"][192:512, 256:768], r_["kc_l"][192:512, 256:768] = split(r_["kt"][...])
        for n in ("kc_h", "kc_l"):
            r_[n][0:192, 256:768] = jnp.zeros((192, 512), BF16)
            r_[n][192:512, 0:256] = jnp.zeros((320, 256), BF16)

    updated = stage(0, first, product(dot_t, "wc"), prepare, lambda value, h: value, "kc")
    moved = to_owners("tu", eight(updated[:, 0:256]), eight(updated[:, 256:768]))
    for c in indices:
        c.wait_recv()
    landing = pieces("ti", indices, 0, 48)
    r_["land"][...] = (iota((1024, 768), 0) == landing[0:1, :].astype(jnp.int32)).astype(F32).astype(BF16)
    for c in moved:
        c.wait_recv()
    arrived = exact(dot_t, pieces("tu", moved, 0, 48), "land")

    loads["cp"].wait()
    r_["ag1"][chip] = r_["cp"][...] - arrived[0:6]
    first = gather_start(1)
    loads["ip"].wait()
    r_["wp_h"][...], r_["wp_l"][...] = split(r_["ip"][...])
    parent = stage(1, first, product(dot_t, "wp"), lambda: None, lambda value, h: value, "wp")
    out[:, 1024:2048] = parent

    picked = exact(dot, eight(parent), "land")
    for d in range(16):
        r_["tb"][d, :, 0:48] = picked[:, 48 * d : 48 * d + 48]
    moved = exchange("tb")
    for c in moved:
        c.wait_recv()
    r_["ag2"][chip, :, 0:256] = exact(dot, pieces("tb", moved, 0, 16), "c1")[0:6]
    r_["ag2"][chip, :, 256:768] = exact(dot, pieces("tb", moved, 16, 48), "c2")[0:6]
    first = gather_start(2)
    reduced = lambda value, h: shared(f"0{h}") - value
    out[:, 0:1024] = stage(2, first, product(dot_t, "kc"), lambda: None, reduced, "wc")

    for c in sent:
        c.wait_send()


def parts(whole, one, two, parent):
    one[...] = whole[:, 0:384]
    two[...] = whole[:, 384:1024]
    parent[...] = whole[:, 1024:2048]


def local(co, ct, cp, io, it, ip, ko, kt, m1, m2):
    vmem, hbm = pl.BlockSpec(memory_space=pltpu.VMEM), pl.BlockSpec(memory_space=pl.ANY)
    shape = lambda like: jax.ShapeDtypeStruct(like.shape, F32)
    whole = pl.pallas_call(
        kernel,
        name="fronts",
        out_shape=jax.ShapeDtypeStruct((6, 2048), F32),
        in_specs=[hbm] * 10,
        out_specs=vmem,
        scratch_shapes=[PLAN[n] for n in NAMES],
        compiler_params=pltpu.CompilerParams(collective_id=1, has_side_effects=True, vmem_limit_bytes=58 * 2**20),
    )(co, ct, cp, io, it, ip, ko, kt, m1.reshape(16, 1, 256), m2.reshape(16, 1, 512))
    return pl.pallas_call(
        parts,
        name="parts",
        out_shape=(shape(co), shape(ct), shape(cp)),
        in_specs=[vmem],
        out_specs=(vmem,) * 3,
    )(whole)


def solution(mesh):
    block = P("front", "col")
    return jax.shard_map(
        local,
        mesh=mesh,
        in_specs=(block,) * 8 + (P(), P()),
        out_specs=(block,) * 3,
        check_vma=False,
    )
```

```python
import functools

import jax
import jax.numpy as jnp
from jax import lax
from jax.experimental import pallas as pl
from jax.experimental.pallas import tpu as pltpu
from jax.sharding import PartitionSpec as P

MESH = pl.DeviceIdType.MESH
F32, BF16 = jnp.float32, jnp.bfloat16
CHIPS = [(dy, dx) for dy in range(4) for dx in range(4) if (dy, dx) != (0, 0)]
CHIPS.sort(key=lambda o: -(min(o[0], 4 - o[0]) + min(o[1], 4 - o[1])))
Z_ORDER = sorted(range(1, 16), key=lambda d: -min(d, 16 - d))


def split(value):
    high = value.astype(BF16)
    return high, (value - high.astype(F32)).astype(BF16)


def dot(left, right):
    return lax.dot_general(left, right, (((1,), (0,)), ((), ())), preferred_element_type=F32)


def dot_t(left, right):
    return lax.dot_general(left, right, (((1,), (1,)), ((), ())), preferred_element_type=F32)


def three(dot_fn, left, right):
    (lh, ll), (rh, rl) = left, right
    rows = lh.shape[0]
    both = dot_fn(jnp.concatenate([lh, ll], axis=0), rh)
    return both[0:rows] + (both[rows : 2 * rows] + dot_fn(lh, rl))


def iota(shape, dim):
    return lax.broadcasted_iota(jnp.int32, shape, dim)


COLUMNS = {"wc": ((0, 1024), (384, 1024)), "kc": ((0, 768), (256, 768)), "wp": ((0, 1024), (0, 1024))}
ROWS = {"wc": ((0, 256), (0, 512), (128, 512), (128, 512)), "kc": ((0, 256), (128, 512), (128, 512)), "wp": ((0, 512),) * 4}


def scratch_plan():
    plan = {}
    vm = lambda *shape: pltpu.VMEM(shape, F32)
    half = lambda *shape: pltpu.VMEM(shape, BF16)
    dma = lambda *shape: pltpu.SemaphoreType.DMA(shape)
    for name, shape in (("io", (192, 384)), ("it", (320, 640)), ("ip", (512, 1024)), ("ko", (192, 256)), ("kt", (320, 512))):
        plan[name] = vm(*shape)
    plan["cp"], plan["m1"], plan["m2"] = vm(6, 1024), pltpu.VMEM((1, 256), jnp.int32), pltpu.VMEM((1, 512), jnp.int32)
    plan["load"] = dma(10)
    for name, shape in (("wc", (512, 1024)), ("wp", (512, 1024)), ("kc", (512, 768))):
        plan[name + "_h"] = half(*shape)
        plan[name + "_l"] = half(*shape)
    plan["c1"], plan["c2"], plan["land"] = half(256, 256), half(512, 512), half(1024, 768)
    for n in ("ti", "tu", "tb"):
        plan[n], plan[n + "g"] = vm(16, 8, 128), vm(16, 8, 128)
        plan[n + "_s"], plan[n + "_r"] = dma(16), dma(16)
    for i, (there, back) in enumerate(((1024, 768), (1024, 1024), (768, 1024))):
        plan[f"ag{i}"], plan[f"x{i}"] = vm(16, 6, there), vm(2, 96, there)
        plan[f"ag{i}_s"], plan[f"ag{i}_r"] = dma(16), dma(16)
        for h in (0, 1):
            j = f"{i}{h}"
            plan["yp" + j], plan["g" + j] = vm(16, 24, 128), vm(16, 24, 128)
            plan["ns" + j], plan["nr" + j], plan["n3" + j] = vm(4, 3, 24, 128), vm(4, 3, 24, 128), vm(24, 128)
            plan["fs" + j], plan["f5" + j], plan["f10" + j] = vm(3, 24, 128), vm(2, 2, 24, 128), vm(2, 24, 128)
            plan["gs" + j], plan["gr" + j] = vm(3, 24, 128), vm(4, 3, 24, 128)
            for n, count in (("n", 5), ("f", 4), ("b", 5)):
                plan[f"{n}{j}_s"], plan[f"{n}{j}_r"] = dma(count), dma(count)
        plan[f"p{i}"], plan[f"cr{i}"] = vm(2, 96, back), vm(96, back)
        plan[f"rs{i}"], plan[f"rr{i}"] = vm(16, 6, back), vm(16, 6, back)
        plan[f"rs{i}_s"], plan[f"rs{i}_r"] = dma(16), dma(16)
        plan[f"cr{i}_s"], plan[f"cr{i}_r"] = dma(4), dma(4)
    return plan


PLAN = scratch_plan()
NAMES = list(PLAN)


def kernel(co, ct, cp, io, it, ip, ko, kt, m1, m2, out, *scratch):
    r_ = dict(zip(NAMES, scratch))
    f, z = lax.axis_index("front"), lax.axis_index("col")
    core, chip = f % 2, f // 2
    x, y = chip % 4, chip // 4
    sent = []

    def copy(src, dst, send, recv, device):
        c = pltpu.make_async_remote_copy(
            src_ref=src, dst_ref=dst, send_sem=send, recv_sem=recv, device_id=device, device_id_type=MESH
        )
        c.start()
        sent.append(c)
        return c

    def at_chip(offset):
        other = ((y + offset[0]) % 4) * 4 + (x + offset[1]) % 4
        return other, (other * 2 + core, z)

    def product(dot_fn, left, name, n):
        start, stop = (ROWS if dot_fn is dot else COLUMNS)[name][n]
        inner, outer = slice(start, stop), slice(256 * n, 256 * n + 256)
        at = (inner, outer) if dot_fn is dot else (outer, inner)
        return three(dot_fn, (left[0][:, inner], left[1][:, inner]), (r_[name + "_h"][at], r_[name + "_l"][at]))

    sibling = (chip * 2 + (1 - core), z)

    def at_z(step):
        return (f, (z + step + 16) % 16)

    barrier = pltpu.get_barrier_semaphore()
    pl.semaphore_signal(barrier, inc=1, device_id=sibling, device_id_type=MESH)
    for o in CHIPS:
        pl.semaphore_signal(barrier, inc=1, device_id=at_chip(o)[1], device_id_type=MESH)
    for d in Z_ORDER:
        pl.semaphore_signal(barrier, inc=1, device_id=at_z(d), device_id_type=MESH)

    loads = {}
    ag0 = r_["ag0"]
    for i, (name, ref, to) in enumerate(
        (
            ("co", co, ag0.at[chip, :, 0:384]),
            ("ct", ct, ag0.at[chip, :, 384:1024]),
            ("m1", m1.at[z], r_["m1"]),
            ("m2", m2.at[z], r_["m2"]),
            ("io", io, r_["io"]),
            ("it", it, r_["it"]),
            ("ko", ko, r_["ko"]),
            ("kt", kt, r_["kt"]),
            ("cp", cp, r_["cp"]),
            ("ip", ip, r_["ip"]),
        )
    ):
        loads[name] = pltpu.make_async_copy(ref, to, r_["load"].at[i])
        loads[name].start()

    def order(mapped, width, name):
        share = width // 16
        target = lax.shift_right_logical(mapped, 10)
        marks = (iota((16, width), 0) == target).astype(F32)
        below = (iota((width, width), 0) < iota((width, width), 1)).astype(F32).astype(BF16)
        ranking = jnp.sum(dot(marks.astype(BF16), below) * marks, axis=0, keepdims=True)
        place = target * share + ranking.astype(jnp.int32)
        r_[name][...] = (iota((width, width), 0) == place).astype(F32).astype(BF16)
        position = jnp.bitwise_and(mapped, 1023).astype(F32)
        return jnp.where(iota((8, width), 0) == 0, position, 0.0)

    def exact(dot_fn, value, name):
        high = value.astype(BF16).astype(F32)
        both = dot_fn(jnp.concatenate([high, value - high], axis=0).astype(BF16), r_[name][...])
        return both[0:8] + both[8:16]

    def exchange(n):
        tiles = r_[n]
        r_[n + "g"][z] = tiles[z]
        return [
            copy(tiles.at[(z + d) % 16], r_[n + "g"].at[z], r_[n + "_s"].at[k], r_[n + "_r"].at[k], at_z(d))
            for k, d in enumerate(Z_ORDER)
        ]

    def to_owners(n, one, two):
        tiles = r_[n]
        for value, name, share, at in ((one, "c1", 16, 0), (two, "c2", 32, 16)):
            ordered = exact(dot_t, value, name)
            for d in range(16):
                tiles[d, :, at : at + share] = ordered[:, share * d : share * d + share]
        return exchange(n)

    def pieces(n, copies, start, stop):
        return jnp.concatenate([r_[n + "g"][k][:, start:stop] for k in range(16)], axis=1)

    loads["co"].wait()
    loads["ct"].wait()

    pl.semaphore_wait(barrier, 31)

    def gather_start(i):
        buf = r_[f"ag{i}"]
        return [
            copy(buf.at[chip], buf.at[chip], r_[f"ag{i}_s"].at[k], r_[f"ag{i}_r"].at[k], at_chip(o)[1])
            for k, o in enumerate(CHIPS)
        ]

    def gather_end(i, copies):
        buf, xs = r_[f"ag{i}"], r_[f"x{i}"]
        for c in copies:
            c.wait_recv()
        for j in range(16):
            xs[0, 6 * j : 6 * j + 6, :] = buf[j]
        return copy(xs.at[0], xs.at[1], r_[f"ag{i}_s"].at[15], r_[f"ag{i}_r"].at[15], sibling)

    NEAR = (2, 14, 1, 15)
    odd = z % 2
    opposite = 3 - 6 * odd

    def block(step, j):
        return (z + step + 5 * (j - 1) + 32) % 16

    def share_start(i, value):
        yp = r_["yp" + i]
        for k in range(4):
            yp[4 * k : 4 * k + 4] = value[:, 128 * k : 128 * k + 128].reshape(4, 24, 128)
        ns, nr = r_["ns" + i], r_["nr" + i]
        sems = lambda k: (r_[f"n{i}_s"].at[k], r_[f"n{i}_r"].at[k])
        near = [copy(yp.at[(z + 8) % 16], r_["n3" + i], *sems(4), at_z(opposite))]
        for k, n in enumerate(NEAR):
            for j in range(3):
                ns[k, j] = yp[block(n, j)]
            near.append(copy(ns.at[k], nr.at[k], *sems(k), at_z(n)))
        return near

    def share(i, near):
        yp, nr, fs, f5, f10 = r_["yp" + i], r_["nr" + i], r_["fs" + i], r_["f5" + i], r_["f10" + i]
        g, gs, gr = r_["g" + i], r_["gs" + i], r_["gr" + i]
        yield
        for c in near:
            c.wait_recv()
        for j in range(3):
            fs[j] = yp[block(0, j)] + ((nr[0, j] + nr[1, j]) + (nr[2, j] + nr[3, j]))
        fs[2 * odd] = fs[2 * odd] + r_["n3" + i][...]
        sems = lambda k: (r_[f"f{i}_s"].at[k], r_[f"f{i}_r"].at[k])
        far = [
            copy(fs.at[2], f10.at[0], *sems(0), at_z(10)),
            copy(fs.at[0], f10.at[1], *sems(1), at_z(-10)),
            copy(fs.at[pl.ds(1, 2)], f5.at[0], *sems(2), at_z(5)),
            copy(fs.at[pl.ds(0, 2)], f5.at[1], *sems(3), at_z(-5)),
        ]
        yield
        for c in far:
            c.wait_recv()
        gs[0] = fs[0] + (f5[0, 0] + f10[0])
        gs[1] = fs[1] + (f5[0, 1] + f5[1, 0])
        gs[2] = fs[2] + (f5[1, 1] + f10[1])
        sent_sems = lambda k: (r_[f"b{i}_s"].at[k], r_[f"b{i}_r"].at[k])
        near = [copy(gs.at[2 * odd], g.at[block(0, 2 * odd)], *sent_sems(4), at_z(opposite))]
        near += [copy(gs, gr.at[k], *sent_sems(k), at_z(n)) for k, n in enumerate(NEAR)]
        for j in range(3):
            g[block(0, j)] = gs[j]
        yield
        for c in near:
            c.wait_recv()
        for k, n in enumerate(NEAR):
            for j in range(3):
                g[block(-n, j)] = gr[k, j]

    def shared(i):
        g = r_["g" + i]
        return jnp.concatenate([g[4 * k : 4 * k + 4].reshape(96, 128) for k in range(4)], axis=1)

    def stage(i, first, there, meanwhile, take, back):
        xs, p, cr, rs, rr = r_[f"x{i}"], r_[f"p{i}"], r_[f"cr{i}"], r_[f"rs{i}"], r_[f"rr{i}"]
        def forth(value):
            value = split(value)
            return jnp.concatenate([product(dot_t, value, there, n) for n in range(2)], axis=1)

        across = gather_end(i, first)
        left = share(f"{i}0", share_start(f"{i}0", forth(xs[0])))
        next(left)
        across.wait_recv()
        right = share(f"{i}1", share_start(f"{i}1", forth(xs[1])))
        meanwhile()
        next(right)
        for _ in range(2):
            next(left)
            next(right)
        for _ in left:
            pass
        value = split(take(shared(f"{i}0"), 0))
        for c in range(p.shape[2] // 256):
            p[0, :, 256 * c : 256 * c + 256] = product(dot, value, back, c)
        for _ in right:
            pass
        value, across = split(take(shared(f"{i}1"), 1)), []
        for c in range(p.shape[2] // 256):
            part = (slice(None), slice(256 * c, 256 * c + 256))
            p[(1,) + part] = product(dot, value, back, c)
            across.append(copy(p.at[(1,) + part], cr.at[part], r_[f"cr{i}_s"].at[c], r_[f"cr{i}_r"].at[c], sibling))
        for c in across:
            c.wait_recv()
        for j in range(16):
            rs[j] = p[0, 6 * j : 6 * j + 6, :] + cr[6 * j : 6 * j + 6, :]
        copies = [
            copy(rs.at[at_chip(o)[0]], rr.at[k], r_[f"rs{i}_s"].at[k], r_[f"rs{i}_r"].at[k], at_chip(o)[1])
            for k, o in enumerate(CHIPS)
        ]
        total = rs[chip]
        for k, c in enumerate(copies):
            c.wait_recv()
            total = total + rr[k]
        return total

    first = gather_start(0)
    loads["m1"].wait()
    loads["m2"].wait()
    index_one = order(r_["m1"][...], 256, "c1")
    index_two = order(r_["m2"][...], 512, "c2")
    indices = to_owners("ti", index_one, index_two)
    eight = lambda value: jnp.concatenate([value, jnp.zeros((2, value.shape[1]), F32)], axis=0)

    for name in ("wc_h", "wc_l"):
        r_[name][0:192, 384:1024] = jnp.zeros((192, 640), BF16)
        r_[name][192:512, 0:384] = jnp.zeros((320, 384), BF16)
    loads["io"].wait()
    r_["wc_h"][0:192, 0:384], r_["wc_l"][0:192, 0:384] = split(r_["io"][...])
    loads["it"].wait()
    r_["wc_h"][192:512, 384:1024], r_["wc_l"][192:512, 384:1024] = split(r_["it"][...])

    def prepare():
        loads["ko"].wait()
        loads["kt"].wait()
        r_["kc_h"][0:192, 0:256], r_["kc_l"][0:192, 0:256] = split(r_["ko"][...])
        r_["kc_h"][192:512, 256:768], r_["kc_l"][192:512, 256:768] = split(r_["kt"][...])
        for n in ("kc_h", "kc_l"):
            r_[n][0:192, 256:768] = jnp.zeros((192, 512), BF16)
            r_[n][192:512, 0:256] = jnp.zeros((320, 256), BF16)

    updated = stage(0, first, "wc", prepare, lambda value, h: value, "kc")
    moved = to_owners("tu", eight(updated[:, 0:256]), eight(updated[:, 256:768]))
    for c in indices:
        c.wait_recv()
    landing = pieces("ti", indices, 0, 48)
    r_["land"][...] = (iota((1024, 768), 0) == landing[0:1, :].astype(jnp.int32)).astype(F32).astype(BF16)
    for c in moved:
        c.wait_recv()
    arrived = exact(dot_t, pieces("tu", moved, 0, 48), "land")

    loads["cp"].wait()
    r_["ag1"][chip] = r_["cp"][...] - arrived[0:6]
    first = gather_start(1)
    loads["ip"].wait()
    r_["wp_h"][...], r_["wp_l"][...] = split(r_["ip"][...])
    parent = stage(1, first, "wp", lambda: None, lambda value, h: value, "wp")
    out[:, 1024:2048] = parent

    picked = exact(dot, eight(parent), "land")
    for d in range(16):
        r_["tb"][d, :, 0:48] = picked[:, 48 * d : 48 * d + 48]
    moved = exchange("tb")
    for c in moved:
        c.wait_recv()
    r_["ag2"][chip, :, 0:256] = exact(dot, pieces("tb", moved, 0, 16), "c1")[0:6]
    r_["ag2"][chip, :, 256:768] = exact(dot, pieces("tb", moved, 16, 48), "c2")[0:6]
    first = gather_start(2)
    reduced = lambda value, h: shared(f"0{h}") - value
    out[:, 0:1024] = stage(2, first, "kc", lambda: None, reduced, "wc")

    for c in sent:
        c.wait_send()


def parts(whole, one, two, parent):
    one[...] = whole[:, 0:384]
    two[...] = whole[:, 384:1024]
    parent[...] = whole[:, 1024:2048]


def local(co, ct, cp, io, it, ip, ko, kt, m1, m2):
    vmem, hbm = pl.BlockSpec(memory_space=pltpu.VMEM), pl.BlockSpec(memory_space=pl.ANY)
    shape = lambda like: jax.ShapeDtypeStruct(like.shape, F32)
    whole = pl.pallas_call(
        kernel,
        name="fronts",
        out_shape=jax.ShapeDtypeStruct((6, 2048), F32),
        in_specs=[hbm] * 10,
        out_specs=vmem,
        scratch_shapes=[PLAN[n] for n in NAMES],
        compiler_params=pltpu.CompilerParams(collective_id=1, has_side_effects=True, vmem_limit_bytes=58 * 2**20),
    )(co, ct, cp, io, it, ip, ko, kt, m1.reshape(16, 1, 256), m2.reshape(16, 1, 512))
    return pl.pallas_call(
        parts,
        name="parts",
        out_shape=(shape(co), shape(ct), shape(cp)),
        in_specs=[vmem],
        out_specs=(vmem,) * 3,
    )(whole)


def solution(mesh):
    block = P("front", "col")
    return jax.shard_map(
        local,
        mesh=mesh,
        in_specs=(block,) * 8 + (P(), P()),
        out_specs=(block,) * 3,
        check_vma=False,
    )
```
